512 devices in a mesh: dp: 64 (over z_hi, x, y), tensor: 8 (over z_lo, core).
Axes of the slice: x: 4, y: 4, z: 16 (z_hi: 4, z_lo: 4; z = z_hi * 4 + z_lo), core: 2. Of those that a mesh axis runs over, the one named last changes fastest.
Arguments:
- hidden_act: bfloat16 [16384, 1152], P('dp', 'tensor'), may hold values from -6 to 6
- out_grad: bfloat16 [16384, 5120], P('dp', 'tensor'), may hold values from -0.375 to 0.375
- error_in: bfloat16 [64, 1152, 5120], P('dp', 'tensor'), may hold values from -6 to 6
- subspace: bfloat16 [5120, 256], P('tensor', 'dp'), may hold values from -0.078125 to 0.078125
- first_moment: float32 [1152, 256], P('tensor', 'dp'), may hold values from -1.8 to 1.8
- second_moment: float32 [1152, 256], P('tensor', 'dp'), may hold values from 0.0001 to 0.01
Outputs:
- weight_step: bfloat16 [1152, 5120], P('tensor')
- error_out: bfloat16 [64, 1152, 5120], P('dp', 'tensor')
- first_new: float32 [1152, 256], P('tensor', 'dp')
- second_new: float32 [1152, 256], P('tensor', 'dp')
The draws below stay inside these ranges and needn't reach their ends.
All inputs are finite; a program needn't handle non-finite values.
Results may differ from the reference program's by a relative error of at most 0.0095.
Values may be sent and summed in bfloat16 or wider, within the bound.
No kernel may reach another device: no remote copies, remote signals or barrier semaphores. Data moves between devices by JAX's collectives and lax.ppermute only.
A program may use at most 64 MiB of HBM per device.

```python
import math
import jax
import jax.numpy as jnp
from jax import lax

D = 5120
R = 256
STEP = 20
TOK_DEV = 256
WROWS = 1152
TOKENS = 16384
REPLICAS = 64
N_DP = 64


def block_scale(stream_key, extent, shards, smallest, largest):
    factor_of, own = 1.0, jax.random.fold_in(stream_key, 6)
    for dim, blocks in shards:
        heights = jnp.exp(jax.random.uniform(jax.random.fold_in(own, dim), (blocks,), jnp.float32, smallest / len(shards), largest / len(shards)))
        factor_of = factor_of * jnp.repeat(heights, extent[dim] // blocks).reshape([-1 if axis == dim else 1 for axis in range(len(extent))])
    return factor_of


def normal_values(key, shape, width, reach, pieces=(), dtype=jnp.bfloat16):
    values = jax.random.normal(key, shape, jnp.float32) * width
    if len(pieces) > 0:
        values = block_scale(key, shape, pieces, -0.22, 0.18) * values
    return jnp.clip(values, min=-reach, max=reach).astype(dtype)


def setup_inputs(seed: int = 0) -> dict:
    key_list = jax.random.split(jax.random.key(seed), 7)
    return {
        "hidden_act": normal_values(key_list[0], (TOKENS, WROWS), 1.0, 6.0, ((0, 64), (1, 8))),
        "out_grad": normal_values(key_list[1], (TOKENS, D), (TOK_DEV ** -0.5), 0.375, ((0, 64), (1, 8))),
        "error_in": normal_values(key_list[2], (REPLICAS, WROWS, D), 1.0, 6.0, ((0, 64), (1, 8))),
        "subspace": normal_values(key_list[3], (D, R), D ** -0.5, 0.078125, ((0, 8), (1, 64))),
        "first_moment": normal_values(key_list[4], (WROWS, R), 0.3, 1.8, ((0, 8), (1, 64)), jnp.float32),
        "second_moment": jnp.clip(jnp.exp(math.log(0.01) - 4.6051702 * jax.random.uniform(key_list[5], (WROWS, R), jnp.float32) ** block_scale(key_list[5], (WROWS, R), ((0, 8), (1, 64)), -0.2, 0.2)), 0.0001, 0.01),
    }


BETA_ONE = 0.9
BETA_TWO = 0.999
EPSILON = 1e-08

def reference(hidden_act, out_grad, error_in, subspace, first_moment, second_moment):
    basis_wide = subspace.astype(jnp.float32)
    inputs_all = hidden_act.reshape(N_DP, TOK_DEV, WROWS)
    grads_all = out_grad.reshape(N_DP, TOK_DEV, D)

    def replica(triple):
        inputs, grads, errors = triple
        gradient = jnp.dot(inputs.T, grads, preferred_element_type=jnp.float32).astype(jnp.bfloat16)
        accumulated = gradient.astype(jnp.float32) + errors.astype(jnp.float32)
        projected = jnp.dot(accumulated, basis_wide, precision=lax.Precision.HIGHEST)
        back = jnp.dot(projected, basis_wide.T, precision=lax.Precision.HIGHEST)
        return (projected, (accumulated - back).astype(jnp.bfloat16))
    projected_all, error_out = lax.map(replica, (inputs_all, grads_all, error_in))
    mean_proj = lax.optimization_barrier(jnp.mean(projected_all, axis=0))
    first_new = BETA_ONE * first_moment + (1.0 - BETA_ONE) * mean_proj
    second_new = BETA_TWO * second_moment + (1.0 - BETA_TWO) * mean_proj * mean_proj
    first_hat = first_new / (1.0 - BETA_ONE ** STEP)
    second_hat = second_new / (1.0 - BETA_TWO ** STEP)
    update = (first_hat / (jnp.sqrt(second_hat) + EPSILON)).astype(jnp.bfloat16)
    weight_step = jnp.dot(update, subspace.T, preferred_element_type=jnp.float32).astype(jnp.bfloat16)
    return (weight_step, error_out, first_new, second_new)
```

```python
import jax
import jax.numpy as jnp
from jax import lax
from jax.experimental import pallas as pl
from jax.experimental.pallas import tpu as pltpu
from jax.sharding import Mesh, PartitionSpec as P

STEP = 20
BETA_ONE = 0.9
BETA_TWO = 0.999
EPSILON = 1e-08

AXES = ("zh", "x", "y", "zl", "c")
SIZES = (4, 4, 4, 4, 2)
DP = ("zh", "x", "y")
TENSOR = ("zl", "c")
ROWS, WIDTH, RANK, TOKENS = 144, 640, 256, 256
COLUMNS = 8 * WIDTH
VMEM = 60 * 1024 * 1024
LONG = 60_000_000_000
SHORT = 1_000_000_000
LONG_MERGE = 3_000_000_000
LONG_UPDATE = 17_000_000_000
LONG_FEEDBACK = 10_000_000_000
LONG_GRADIENTS = 9_200_000_000
f32, bf16 = jnp.float32, jnp.bfloat16


def to_all(block, axes, size):
    return lax.all_to_all(jnp.broadcast_to(block[None], (size, *block.shape)), axes, 0, 0)


def swap_cores(block):
    return lax.ppermute(block, "c", [(0, 1), (1, 0)])


def from_xor(block, bits):
    return lax.ppermute(block, "zl", [(i, i ^ bits) for i in range(4)])


def halves(value):
    high = value.astype(bf16)
    return high, (value - high.astype(f32)).astype(bf16)


def call(kernel, name, out_shape, in_specs, out_specs, scratch, cycles):
    return pl.pallas_call(
        kernel,
        out_shape=out_shape,
        in_specs=in_specs,
        out_specs=out_specs,
        scratch_shapes=scratch,
        compiler_params=pltpu.CompilerParams(vmem_limit_bytes=VMEM),
        cost_estimate=pl.CostEstimate(flops=cycles, bytes_accessed=4_000_000, transcendentals=0),
        name=name,
    )


VM, SM, ANY = pl.BlockSpec(memory_space=pltpu.VMEM), pl.BlockSpec(memory_space=pltpu.SMEM), pl.BlockSpec(memory_space=pl.ANY)
CONTRACT = (((1,), (1,)), ((), ()))
BASIS = (16, 4, 16, WIDTH)


def spread_kernel(along_z, out):
    for zl in range(4):
        block = jnp.concatenate([along_z[zh, zl].astype(f32) for zh in range(4)], axis=0).astype(bf16)
        for peer in range(16):
            out[peer, zl] = block


def spread(along_z):
    return call(
        spread_kernel, "spread", jax.ShapeDtypeStruct(BASIS, bf16), [VM], VM, [], LONG
    )(along_z)


def pick_kernel(place, error, out, held, sems, done):
    copies, outs = [], []
    for z in range(4):
        start = pl.multiple_of((2 * z + 1 - place[1]) * WIDTH, 128)
        copies.append(pltpu.make_async_copy(error.at[:, pl.ds(start, WIDTH)], held.at[z], sems.at[z]))
        copies[z].start()
    for z in range(4):
        copies[z].wait()
        outs.append(pltpu.make_async_copy(held.at[z], out.at[z], done.at[z]))
        outs[z].start()
    for copy in outs:
        copy.wait()


def pick(place, error):
    shape = jax.ShapeDtypeStruct((4, ROWS, WIDTH), bf16)
    scratch = [
        pltpu.VMEM((4, ROWS, WIDTH), bf16),
        pltpu.SemaphoreType.DMA((4,)),
        pltpu.SemaphoreType.DMA((4,)),
    ]
    return call(pick_kernel, "pick", shape, [SM, ANY], ANY, scratch, SHORT)(place, error)


ORDER = (0, 1, 2, 3)


def arrived_kernel(first, second, out):
    out[...] = jnp.zeros_like(out)


def arrived(first, second):
    shape = jax.ShapeDtypeStruct((8, 128), f32)
    return call(arrived_kernel, "arrived", shape, [ANY, ANY], VM, [], LONG_GRADIENTS)(first, second)


def accumulate_kernel(
    place, act, act_other, first, second, third, fourth, ready, error, error_other,
    out, acts, grads, errors, totals, sems, pair_sems, done,
):
    zl, core = place[0], place[1]
    heads = [
        pltpu.make_async_copy(act, acts.at[0], pair_sems.at[0]),
        pltpu.make_async_copy(act_other, acts.at[1], pair_sems.at[1]),
    ]
    for copy in heads:
        copy.start()
    copies = []
    for step, source in enumerate((first, second, third, fourth)):
        z = zl ^ ORDER[step]
        start = pl.multiple_of((2 * z + core) * WIDTH, 128)
        moved = [
            pltpu.make_async_copy(source, grads.at[step], sems.at[step, 0]),
            pltpu.make_async_copy(error.at[:, pl.ds(start, WIDTH)], errors.at[0, step], sems.at[step, 1]),
            pltpu.make_async_copy(error_other.at[z], errors.at[1, step], sems.at[step, 2]),
        ]
        for copy in moved:
            copy.start()
        copies.append(moved)
    for copy in heads:
        copy.wait()
    outs = []
    for step in range(4):
        for copy in copies[step]:
            copy.wait()
        for side in range(2):
            gradient = jnp.dot(acts[side], grads[step], preferred_element_type=f32).astype(bf16)
            high, low = halves(gradient.astype(f32) + errors[side, step].astype(f32))
            totals[step, side] = jnp.concatenate([high, low], axis=0)
            outs.append(pltpu.make_async_copy(totals.at[step, side], out.at[step, side], done.at[step, side]))
            outs[-1].start()
    for copy in outs:
        copy.wait()


def accumulate(place, act, act_other, grads, ready, error, error_other):
    return call(
        accumulate_kernel,
        "accumulate",
        jax.ShapeDtypeStruct((4, 2, 2 * ROWS, WIDTH), bf16),
        [SM] + [ANY] * 9,
        ANY,
        [
            pltpu.VMEM((2, ROWS, TOKENS), bf16),
            pltpu.VMEM((4, TOKENS, WIDTH), bf16),
            pltpu.VMEM((2, 4, ROWS, WIDTH), bf16),
            pltpu.VMEM((4, 2, 2 * ROWS, WIDTH), bf16),
            pltpu.SemaphoreType.DMA((4, 3)),
            pltpu.SemaphoreType.DMA((2,)),
            pltpu.SemaphoreType.DMA((4, 2)),
        ],
        SHORT,
    )(place, act, act_other, *grads, ready, error, error_other)


def project_kernel(place, total, own, turned, sums, totals, basis, sems):
    zl, core = place[0], place[1]
    copies = []
    for step in range(4):
        z = zl ^ ORDER[step]
        moved = [
            pltpu.make_async_copy(total.at[step], totals.at[step], sems.at[step, 0]),
            pltpu.make_async_copy(own.at[:, z], basis.at[step], sems.at[step, 1]),
        ]
        for copy in moved:
            copy.start()
        copies.append(moved)
    values = [jnp.zeros((2 * ROWS, RANK), f32)] * 2
    for step in range(4):
        for copy in copies[step]:
            copy.wait()
        part = basis[step].reshape(RANK, WIDTH)
        for side in range(2):
            values[side] += lax.dot_general(totals[step, side], part, CONTRACT, preferred_element_type=f32)
    for side in range(2):
        projected = values[side][:ROWS] + values[side][ROWS:]
        sums[side] = projected
        padded = jnp.concatenate([projected, jnp.zeros((RANK - ROWS, RANK), f32)], axis=0)
        turned[1 - core if side else core] = padded.T[:, :ROWS].astype(bf16)


def project(place, total, own):
    return call(
        project_kernel,
        "project",
        (jax.ShapeDtypeStruct((2, RANK, ROWS), bf16), jax.ShapeDtypeStruct((2, ROWS, RANK), f32)),
        [SM, ANY, ANY],
        (VM, VM),
        [
            pltpu.VMEM((4, 2, 2 * ROWS, WIDTH), bf16),
            pltpu.VMEM((4, 16, 16, WIDTH), bf16),
            pltpu.SemaphoreType.DMA((4, 2)),
        ],
        SHORT,
    )(place, total, own)


def feedback_kernel(
    place, total, sums, received, own, kept, sent, totals, basis, results, sems, done
):
    zl = place[0]
    copies = []
    for step in range(4):
        z = zl ^ ORDER[step]
        moved = [
            pltpu.make_async_copy(total.at[step], totals.at[step], sems.at[step, 0]),
            pltpu.make_async_copy(own.at[:, z], basis.at[step], sems.at[step, 1]),
        ]
        for copy in moved:
            copy.start()
        copies.append(moved)
    backs = []
    for side in range(2):
        backs.append(jnp.concatenate(halves(sums[side] + received[1 - side]), axis=0))
    outs = []
    for step in range(4):
        for copy in copies[step]:
            copy.wait()
        part = basis[step].reshape(RANK, WIDTH)
        for side, target in ((1, sent), (0, kept)):
            back = jnp.dot(backs[side], part, preferred_element_type=f32)
            value = totals[step, side, :ROWS].astype(f32) + totals[step, side, ROWS:].astype(f32)
            results[side, step] = (value - (back[:ROWS] + back[ROWS:])).astype(bf16)
            outs.append(pltpu.make_async_copy(results.at[side, step], target.at[step], done.at[side, step]))
            outs[-1].start()
    for copy in outs:
        copy.wait()


def feedback(place, total, sums, received, own):
    shape = jax.ShapeDtypeStruct((4, ROWS, WIDTH), bf16)
    return call(
        feedback_kernel,
        "feedback",
        (shape, shape),
        [SM, ANY, VM, VM, ANY],
        (ANY, ANY),
        [
            pltpu.VMEM((4, 2, 2 * ROWS, WIDTH), bf16),
            pltpu.VMEM((4, 16, 16, WIDTH), bf16),
            pltpu.VMEM((2, 4, ROWS, WIDTH), bf16),
            pltpu.SemaphoreType.DMA((4, 2)),
            pltpu.SemaphoreType.DMA((2, 4)),
        ],
        LONG_FEEDBACK,
    )(place, total, sums, received, own)


def merge_kernel(place, kept, received, out, held, sems, done):
    zl, core = place[0], place[1]
    copies, outs = [], []
    for step in range(4):
        z = zl ^ ORDER[step]
        for side, source in enumerate((kept, received)):
            start = pl.multiple_of((2 * z + (1 - core if side else core)) * WIDTH, 128)
            copies.append(pltpu.make_async_copy(source.at[step], held.at[:, pl.ds(start, WIDTH)], sems.at[step, side]))
            copies[-1].start()
    for copy in copies:
        copy.wait()
    for part in range(3):
        rows = pl.ds(part * 48, 48)
        outs.append(pltpu.make_async_copy(held.at[rows], out.at[rows], done.at[part]))
        outs[part].start()
    for copy in outs:
        copy.wait()


def merge(place, kept, received):
    shape = jax.ShapeDtypeStruct((ROWS, COLUMNS), bf16)
    scratch = [
        pltpu.VMEM((ROWS, COLUMNS), bf16),
        pltpu.SemaphoreType.DMA((4, 2)),
        pltpu.SemaphoreType.DMA((3,)),
    ]
    return call(merge_kernel, "merge", shape, [SM, ANY, ANY], ANY, scratch, LONG_MERGE)(place, kept, received)


def weight_kernel(place, updates, own, other, out, held, mine, theirs, results, head, sems, done):
    first = place[1] == 0
    pltpu.make_async_copy(updates, held, head.at[0]).start()
    copies = []
    for z in range(4):
        copies.append(pltpu.make_async_copy(own.at[:, z], mine.at[z], sems.at[z, 0]))
        copies.append(pltpu.make_async_copy(other.at[:, z], theirs.at[z], sems.at[z, 1]))
    for copy in copies:
        copy.start()
    pltpu.make_async_copy(updates, held, head.at[0]).wait()
    value = held[...].reshape(RANK, ROWS).astype(f32)
    padded = jnp.concatenate([value, jnp.zeros((RANK, RANK - ROWS), f32)], axis=1)
    turned = padded.T[:ROWS].astype(bf16)
    outs = []
    for z in range(4):
        copies[2 * z].wait()
        copies[2 * z + 1].wait()
        both = mine[z].reshape(RANK, WIDTH), theirs[z].reshape(RANK, WIDTH)
        for core in range(2):
            part = jnp.where(first, both[core], both[1 - core])
            start = (2 * z + core) * WIDTH
            step = jnp.dot(turned, part, preferred_element_type=f32)
            results[:, start : start + WIDTH] = step.astype(bf16)
        columns = pl.ds(z * 2 * WIDTH, 2 * WIDTH)
        outs.append(pltpu.make_async_copy(results.at[:, columns], out.at[:, columns], done.at[z]))
        outs[z].start()
    for copy in outs:
        copy.wait()


def weight(place, updates, own, other):
    return call(
        weight_kernel,
        "weight_step",
        jax.ShapeDtypeStruct((ROWS, COLUMNS), bf16),
        [SM, ANY, ANY, ANY],
        ANY,
        [
            pltpu.VMEM((16, 16, ROWS), bf16),
            pltpu.VMEM((4, 16, 16, WIDTH), bf16),
            pltpu.VMEM((4, 16, 16, WIDTH), bf16),
            pltpu.VMEM((ROWS, COLUMNS), bf16),
            pltpu.SemaphoreType.DMA((1,)),
            pltpu.SemaphoreType.DMA((4, 2)),
            pltpu.SemaphoreType.DMA((4,)),
        ],
        SHORT,
    )(place, updates, own, other)


def combine_kernel(part, first, second, out):
    total = jnp.sum(part[...].astype(f32), axis=0)
    for peer in range(4):
        out[peer, :16] = total
        out[peer, 16:20] = first[...]
        out[peer, 20:] = second[...]


def combine(part, first, second):
    shape = jax.ShapeDtypeStruct((4, 24, ROWS), f32)
    return call(combine_kernel, "combine", shape, [VM] * 3, VM, [], SHORT)(part, first, second)


def moments(first, second, mean):
    first = BETA_ONE * first + (1.0 - BETA_ONE) * mean
    second = BETA_TWO * second + (1.0 - BETA_TWO) * mean * mean
    return first, second


def update_kernel(place, both, out, first_own, second_own, held):
    mean = (both[0, :16] + both[1, :16] + both[2, :16] + both[3, :16]) / 64
    for peer in range(4):
        held[peer] = mean[4 * peer : 4 * peer + 4]
    first = jnp.concatenate([both[peer, 16:20] for peer in range(4)], axis=0)
    second = jnp.concatenate([both[peer, 20:24] for peer in range(4)], axis=0)
    first, second = moments(first, second, mean)
    first_hat = first / (1.0 - BETA_ONE**STEP)
    second_hat = second / (1.0 - BETA_TWO**STEP)
    update = (first_hat / (jnp.sqrt(second_hat) + EPSILON)).astype(bf16)
    for peer in range(16):
        out[peer] = update
    zh = place[2]
    mine = held[zh]
    first_own[...], second_own[...] = moments(both[zh, 16:20], both[zh, 20:24], mine)


def new_update(place, both):
    shape = jax.ShapeDtypeStruct((4, ROWS), f32)
    return call(
        update_kernel,
        "update",
        (jax.ShapeDtypeStruct((16, 16, ROWS), bf16), shape, shape),
        [SM, VM],
        (VM, VM, VM),
        [pltpu.VMEM((4, 4, ROWS), f32)],
        LONG_UPDATE,
    )(place, both)


def local(hidden_act, out_grad, error_in, subspace, first_moment, second_moment):
    zh = lax.axis_index("zh")
    place = jnp.stack([lax.axis_index("zl"), lax.axis_index("c"), zh]).astype(jnp.int32)
    act = hidden_act.T

    along_z = to_all(subspace.T, ("zh", "zl"), 16)
    spreading = spread(along_z.reshape(4, 4, 4, WIDTH))
    own = lax.all_to_all(spreading, ("x", "y"), 0, 0)
    error = error_in[0]
    grads = [out_grad] + [from_xor(out_grad, bits) for bits in ORDER[1:]]
    error_other = swap_cores(pick(place, error))
    ready = arrived(grads[2], grads[3])
    total = accumulate(place, act, swap_cores(act), grads, ready, error, error_other)
    own, total = lax.optimization_barrier((own, total))
    turned, sums = project(place, total, own)

    part = lax.all_to_all(turned.reshape(32, 16, ROWS), ("c", "x", "y"), 0, 0)
    received = swap_cores(sums)
    error_kept, error_sent = feedback(place, total, sums, received, own)
    part, error_kept, error_sent, later = lax.optimization_barrier((part, error_kept, error_sent, own))
    other = swap_cores(later)
    error_received = swap_cores(error_sent)
    both = combine(part, first_moment.T, second_moment.T)
    both = lax.all_to_all(both, "zh", 0, 0)
    error_received, other = lax.optimization_barrier((error_received, other))
    error_out = merge(place, error_kept, error_received)
    update, first_own, second_own = new_update(place, both)
    updates = lax.all_to_all(update, ("x", "y"), 0, 0)
    weight_step = weight(place, updates, own, other)
    return (weight_step, error_out[None], first_own.T, second_own.T)


def solution(mesh):
    fine = Mesh(mesh.devices.reshape(SIZES), AXES)
    placed = (
        P(DP, TENSOR),
        P(DP, TENSOR),
        P(DP, TENSOR, None),
        P(TENSOR, DP),
        P(TENSOR, DP),
        P(TENSOR, DP),
    )
    return jax.shard_map(
        local,
        mesh=fine,
        in_specs=placed,
        out_specs=(P(TENSOR, None), P(DP, TENSOR, None), P(TENSOR, DP), P(TENSOR, DP)),
        check_vma=False,
    )
```

```python
import jax
import jax.numpy as jnp
from jax import lax
from jax.experimental import pallas as pl
from jax.experimental.pallas import tpu as pltpu
from jax.sharding import Mesh, PartitionSpec as P

STEP = 20
BETA_ONE = 0.9
BETA_TWO = 0.999
EPSILON = 1e-08

AXES = ("zh", "x", "y", "zl", "c")
SIZES = (4, 4, 4, 4, 2)
DP = ("zh", "x", "y")
TENSOR = ("zl", "c")
ROWS, WIDTH, RANK, TOKENS = 144, 640, 256, 256
COLUMNS = 8 * WIDTH
LIMITS = {"project": 50, "feedback": 60, "weight_step": 24, "merge": 60}
LONG = 60_000_000_000
SHORT = 1_000_000_000
LONG_MERGE = 3_000_000_000
LONG_UPDATE = 17_000_000_000
LONG_FEEDBACK = 10_000_000_000
LONG_GRADIENTS = 10_300_000_000
f32, bf16 = jnp.float32, jnp.bfloat16


def to_all(block, axes, size):
    return lax.all_to_all(jnp.broadcast_to(block[None], (size, *block.shape)), axes, 0, 0)


def swap_cores(block):
    return lax.ppermute(block, "c", [(0, 1), (1, 0)])


def from_xor(block, bits):
    return lax.ppermute(block, "zl", [(i, i ^ bits) for i in range(4)])


def halves(value):
    high = value.astype(bf16)
    return high, (value - high.astype(f32)).astype(bf16)


def call(kernel, name, out_shape, in_specs, out_specs, scratch, cycles):
    return pl.pallas_call(
        kernel,
        out_shape=out_shape,
        in_specs=in_specs,
        out_specs=out_specs,
        scratch_shapes=scratch,
        compiler_params=pltpu.CompilerParams(vmem_limit_bytes=LIMITS.get(name, 8) * 1024 * 1024),
        cost_estimate=pl.CostEstimate(flops=cycles, bytes_accessed=4_000_000, transcendentals=0),
        name=name,
    )


VM, SM, ANY = pl.BlockSpec(memory_space=pltpu.VMEM), pl.BlockSpec(memory_space=pltpu.SMEM), pl.BlockSpec(memory_space=pl.ANY)
CONTRACT = (((1,), (1,)), ((), ()))
BASIS = (16, 4, 16, WIDTH)


def spread_kernel(along_z, out):
    for zl in range(4):
        block = jnp.concatenate([along_z[zh, zl].astype(f32) for zh in range(4)], axis=0).astype(bf16)
        for peer in range(16):
            out[peer, zl] = block


def spread(along_z):
    return call(
        spread_kernel, "spread", jax.ShapeDtypeStruct(BASIS, bf16), [VM], VM, [], LONG
    )(along_z)


def pick_kernel(place, error, act, out, held, sems, done):
    copies, outs = [], []
    for z in range(4):
        start = pl.multiple_of((2 * z + 1 - place[1]) * WIDTH, 128)
        copies.append(pltpu.make_async_copy(error.at[:, pl.ds(start, WIDTH)], held.at[z], sems.at[z]))
    copies.append(pltpu.make_async_copy(act, held.at[4, :, pl.ds(0, TOKENS)], sems.at[4]))
    for copy in copies:
        copy.start()
    held[4, :, TOKENS:] = jnp.zeros((ROWS, WIDTH - TOKENS), bf16)
    for z in range(5):
        copies[z].wait()
        outs.append(pltpu.make_async_copy(held.at[z], out.at[z], done.at[z]))
        outs[z].start()
    for copy in outs:
        copy.wait()


def pick(place, error, act):
    shape = jax.ShapeDtypeStruct((5, ROWS, WIDTH), bf16)
    scratch = [
        pltpu.VMEM((5, ROWS, WIDTH), bf16),
        pltpu.SemaphoreType.DMA((5,)),
        pltpu.SemaphoreType.DMA((5,)),
    ]
    return call(pick_kernel, "pick", shape, [SM, ANY, ANY], ANY, scratch, SHORT)(place, error, act)


def arrived_kernel(first, second, out):
    out[...] = jnp.zeros_like(out)


def arrived(first, second):
    shape = jax.ShapeDtypeStruct((8, 128), f32)
    return call(arrived_kernel, "arrived", shape, [ANY, ANY], VM, [], LONG_GRADIENTS)(first, second)


def start_basis(source, target, sems):
    copies = [pltpu.make_async_copy(source.at[pl.ds(4 * i, 4)], target.at[pl.ds(4 * i, 4)], sems.at[i]) for i in range(4)]
    for copy in copies:
        copy.start()
    return copies


def project_kernel(
    place, act, picked, first, second, third, fourth, error, own, ready, turned, sums, total,
    acts, grads, errors, basis, totals, sems, basis_sems, act_sems, done,
):
    zl, core = place[0], place[1]
    heads = [
        pltpu.make_async_copy(act, acts.at[0], act_sems.at[0]),
        pltpu.make_async_copy(picked.at[4, :, pl.ds(0, TOKENS)], acts.at[1], act_sems.at[1]),
    ]
    for copy in heads:
        copy.start()
    copies = []
    for bits, source in enumerate((first, second, third, fourth)):
        z = zl ^ bits
        start = pl.multiple_of((2 * z + core) * WIDTH, 128)
        moved = [
            pltpu.make_async_copy(source, grads.at[bits], sems.at[bits, 0]),
            pltpu.make_async_copy(error.at[:, pl.ds(start, WIDTH)], errors.at[0, bits], sems.at[bits, 1]),
            pltpu.make_async_copy(picked.at[z], errors.at[1, bits], sems.at[bits, 2]),
        ]
        for copy in moved:
            copy.start()
        copies.append(moved)
    halves_of_basis = start_basis(own, basis, basis_sems)
    for copy in heads:
        copy.wait()
    outs = []
    for bits in range(4):
        for copy in copies[bits]:
            copy.wait()
        for side in range(2):
            gradient = jnp.dot(acts[side], grads[bits], preferred_element_type=f32).astype(bf16)
            high, low = halves(gradient.astype(f32) + errors[side, bits].astype(f32))
            totals[bits, side, :ROWS] = high
            totals[bits, side, ROWS:] = low
            outs.append(pltpu.make_async_copy(totals.at[bits, side], total.at[zl ^ bits, side], done.at[bits, side]))
            outs[-1].start()
    for copy in halves_of_basis:
        copy.wait()
    values = [jnp.zeros((2 * ROWS, RANK), f32)] * 2
    for bits in range(4):
        part = basis[:, zl ^ bits].reshape(RANK, WIDTH)
        for side in range(2):
            values[side] += lax.dot_general(totals[bits, side], part, CONTRACT, preferred_element_type=f32)
    for side in range(2):
        projected = values[side][:ROWS] + values[side][ROWS:]
        sums[side] = projected
        padded = jnp.concatenate([projected, jnp.zeros((RANK - ROWS, RANK), f32)], axis=0)
        turned[1 - core if side else core] = padded.T[:, :ROWS].astype(bf16)
    for copy in outs:
        copy.wait()


def project(place, act, picked, grads, error, own, ready):
    return call(
        project_kernel,
        "project",
        (
            jax.ShapeDtypeStruct((2, RANK, ROWS), bf16),
            jax.ShapeDtypeStruct((2, ROWS, RANK), f32),
            jax.ShapeDtypeStruct((4, 2, 2 * ROWS, WIDTH), bf16),
        ),
        [SM] + [ANY] * 8 + [VM],
        (VM, VM, ANY),
        [
            pltpu.VMEM((2, ROWS, TOKENS), bf16),
            pltpu.VMEM((4, TOKENS, WIDTH), bf16),
            pltpu.VMEM((2, 4, ROWS, WIDTH), bf16),
            pltpu.VMEM(BASIS, bf16),
            pltpu.VMEM((4, 2, 2 * ROWS, WIDTH), bf16),
            pltpu.SemaphoreType.DMA((4, 3)),
            pltpu.SemaphoreType.DMA((4,)),
            pltpu.SemaphoreType.DMA((2,)),
            pltpu.SemaphoreType.DMA((4, 2)),
        ],
        SHORT,
    )(place, act, picked, *grads, error, own, ready)


def feedback_kernel(total, sums, received, own, kept, sent, totals, basis, results, sems, basis_sems, done):
    halves_of_basis = start_basis(own, basis, basis_sems)
    copies = [pltpu.make_async_copy(total.at[z], totals.at[z], sems.at[z]) for z in range(4)]
    for copy in copies:
        copy.start()
    backs = []
    for side in range(2):
        backs.append(jnp.concatenate(halves(sums[side] + received[1 - side]), axis=0))
    for copy in halves_of_basis:
        copy.wait()
    outs = []
    for z in range(4):
        copies[z].wait()
        part = basis[:, z].reshape(RANK, WIDTH)
        for side, target in ((1, sent), (0, kept)):
            back = jnp.dot(backs[side], part, preferred_element_type=f32)
            value = totals[z, side, :ROWS].astype(f32) + totals[z, side, ROWS:].astype(f32)
            results[side, z] = (value - (back[:ROWS] + back[ROWS:])).astype(bf16)
            outs.append(pltpu.make_async_copy(results.at[side, z], target.at[z], done.at[side, z]))
            outs[-1].start()
    for copy in outs:
        copy.wait()


def feedback(total, sums, received, own):
    shape = jax.ShapeDtypeStruct((4, ROWS, WIDTH), bf16)
    return call(
        feedback_kernel,
        "feedback",
        (shape, shape),
        [ANY, VM, VM, ANY],
        (ANY, ANY),
        [
            pltpu.VMEM((4, 2, 2 * ROWS, WIDTH), bf16),
            pltpu.VMEM(BASIS, bf16),
            pltpu.VMEM((2, 4, ROWS, WIDTH), bf16),
            pltpu.SemaphoreType.DMA((4,)),
            pltpu.SemaphoreType.DMA((4,)),
            pltpu.SemaphoreType.DMA((2, 4)),
        ],
        LONG_FEEDBACK,
    )(total, sums, received, own)


def merge_kernel(place, kept, received, out, held, sems, done):
    core = place[1]
    copies, outs = [], []
    for z in range(4):
        for side, source in enumerate((kept, received)):
            start = pl.multiple_of((2 * z + (1 - core if side else core)) * WIDTH, 128)
            copies.append(pltpu.make_async_copy(source.at[z], held.at[:, pl.ds(start, WIDTH)], sems.at[z, side]))
            copies[-1].start()
    for copy in copies:
        copy.wait()
    for part in range(3):
        rows = pl.ds(part * 48, 48)
        outs.append(pltpu.make_async_copy(held.at[rows], out.at[rows], done.at[part]))
        outs[part].start()
    for copy in outs:
        copy.wait()


def merge(place, kept, received):
    shape = jax.ShapeDtypeStruct((ROWS, COLUMNS), bf16)
    scratch = [
        pltpu.VMEM((ROWS, COLUMNS), bf16),
        pltpu.SemaphoreType.DMA((4, 2)),
        pltpu.SemaphoreType.DMA((3,)),
    ]
    return call(merge_kernel, "merge", shape, [SM, ANY, ANY], ANY, scratch, LONG_MERGE)(place, kept, received)


def weight_kernel(place, updates, own, other, out, held, mine, theirs, results, head, sems, done):
    first = place[1] == 0
    head_copy = pltpu.make_async_copy(updates, held, head.at[0])
    head_copy.start()
    copies = start_basis(own, mine, sems.at[0]) + start_basis(other, theirs, sems.at[1])
    head_copy.wait()
    value = held[...].reshape(RANK, ROWS).astype(f32)
    padded = jnp.concatenate([value, jnp.zeros((RANK, RANK - ROWS), f32)], axis=1)
    turned = padded.T[:ROWS].astype(bf16)
    for copy in copies:
        copy.wait()
    outs = []
    for z in range(4):
        both = mine[:, z].reshape(RANK, WIDTH), theirs[:, z].reshape(RANK, WIDTH)
        for core in range(2):
            part = jnp.where(first, both[core], both[1 - core])
            start = (2 * z + core) * WIDTH
            step = jnp.dot(turned, part, preferred_element_type=f32)
            results[:, start : start + WIDTH] = step.astype(bf16)
        columns = pl.ds(z * 2 * WIDTH, 2 * WIDTH)
        outs.append(pltpu.make_async_copy(results.at[:, columns], out.at[:, columns], done.at[z]))
        outs[z].start()
    for copy in outs:
        copy.wait()


def weight(place, updates, own, other):
    return call(
        weight_kernel,
        "weight_step",
        jax.ShapeDtypeStruct((ROWS, COLUMNS), bf16),
        [SM, ANY, ANY, ANY],
        ANY,
        [
            pltpu.VMEM((16, 16, ROWS), bf16),
            pltpu.VMEM(BASIS, bf16),
            pltpu.VMEM(BASIS, bf16),
            pltpu.VMEM((ROWS, COLUMNS), bf16),
            pltpu.SemaphoreType.DMA((1,)),
            pltpu.SemaphoreType.DMA((2, 4)),
            pltpu.SemaphoreType.DMA((4,)),
        ],
        SHORT,
    )(place, updates, own, other)


def combine_kernel(part, first, second, out):
    total = jnp.sum(part[...].astype(f32), axis=0)
    for peer in range(4):
        out[peer, :16] = total
        out[peer, 16:20] = first[...]
        out[peer, 20:] = second[...]


def combine(part, first, second):
    shape = jax.ShapeDtypeStruct((4, 24, ROWS), f32)
    return call(combine_kernel, "combine", shape, [VM] * 3, VM, [], SHORT)(part, first, second)


def moments(first, second, mean):
    first = BETA_ONE * first + (1.0 - BETA_ONE) * mean
    second = BETA_TWO * second + (1.0 - BETA_TWO) * mean * mean
    return first, second


def update_kernel(place, both, out, first_own, second_own, held):
    mean = (both[0, :16] + both[1, :16] + both[2, :16] + both[3, :16]) / 64
    for peer in range(4):
        held[peer] = mean[4 * peer : 4 * peer + 4]
    first = jnp.concatenate([both[peer, 16:20] for peer in range(4)], axis=0)
    second = jnp.concatenate([both[peer, 20:24] for peer in range(4)], axis=0)
    first, second = moments(first, second, mean)
    first_hat = first / (1.0 - BETA_ONE**STEP)
    second_hat = second / (1.0 - BETA_TWO**STEP)
    update = (first_hat / (jnp.sqrt(second_hat) + EPSILON)).astype(bf16)
    for peer in range(16):
        out[peer] = update
    zh = place[2]
    mine = held[zh]
    first_own[...], second_own[...] = moments(both[zh, 16:20], both[zh, 20:24], mine)


def new_update(place, both):
    shape = jax.ShapeDtypeStruct((4, ROWS), f32)
    return call(
        update_kernel,
        "update",
        (jax.ShapeDtypeStruct((16, 16, ROWS), bf16), shape, shape),
        [SM, VM],
        (VM, VM, VM),
        [pltpu.VMEM((4, 4, ROWS), f32)],
        LONG_UPDATE,
    )(place, both)


def local(hidden_act, out_grad, error_in, subspace, first_moment, second_moment):
    zh = lax.axis_index("zh")
    place = jnp.stack([lax.axis_index("zl"), lax.axis_index("c"), zh]).astype(jnp.int32)
    act = hidden_act.T

    along_z = to_all(subspace.T, ("zh", "zl"), 16)
    spreading = spread(along_z.reshape(4, 4, 4, WIDTH))
    own = lax.all_to_all(spreading, ("x", "y"), 0, 0)
    error = error_in[0]
    error = error_in[0]
    grads = [out_grad] + [from_xor(out_grad, bits) for bits in (1, 2, 3)]
    picked = swap_cores(pick(place, error, act))
    ready = arrived(grads[2], grads[3])
    own, ready, picked, grads[1] = lax.optimization_barrier((own, ready, picked, grads[1]))
    turned, sums, total = project(place, act, picked, grads, error, own, ready)

    part = lax.all_to_all(turned.reshape(32, 16, ROWS), ("c", "x", "y"), 0, 0)
    received = swap_cores(sums)
    error_kept, error_sent = feedback(total, sums, received, own)
    part, error_kept, error_sent, later = lax.optimization_barrier((part, error_kept, error_sent, own))
    other = swap_cores(later)
    error_received = swap_cores(error_sent)
    both = combine(part, first_moment.T, second_moment.T)
    both = lax.all_to_all(both, "zh", 0, 0)
    error_received, other = lax.optimization_barrier((error_received, other))
    error_out = merge(place, error_kept, error_received)
    update, first_own, second_own = new_update(place, both)
    updates = lax.all_to_all(update, ("x", "y"), 0, 0)
    weight_step = weight(place, updates, own, other)
    return (weight_step, error_out[None], first_own.T, second_own.T)


def solution(mesh):
    fine = Mesh(mesh.devices.reshape(SIZES), AXES)
    placed = (
        P(DP, TENSOR),
        P(DP, TENSOR),
        P(DP, TENSOR, None),
        P(TENSOR, DP),
        P(TENSOR, DP),
        P(TENSOR, DP),
    )
    return jax.shard_map(
        local,
        mesh=fine,
        in_specs=placed,
        out_specs=(P(TENSOR, None), P(DP, TENSOR, None), P(TENSOR, DP), P(TENSOR, DP)),
        check_vma=False,
    )
```

```python
import functools

import jax
import jax.numpy as jnp
from jax import lax
from jax.experimental import pallas as pl
from jax.experimental.pallas import tpu as pltpu
from jax.sharding import Mesh, PartitionSpec as P

STEP = 20
BETA_ONE = 0.9
BETA_TWO = 0.999
EPSILON = 1e-08

AXES = ("zh", "x", "y", "zl", "c")
SIZES = (4, 4, 4, 4, 2)
DP = ("zh", "x", "y")
TENSOR = ("zl", "c")
ROWS, WIDTH, RANK, TOKENS = 144, 640, 256, 256
COLUMNS = 8 * WIDTH
LIMITS = {"project": 50, "feedback": 50, "weight_step": 24}
LONG = 60_000_000_000
SHORT = 1_000_000_000
LONG_COMBINE = 17_000_000_000
LONG_UPDATE = 1_000_000_000
LONG_FEEDBACK = 1_000_000_000
LONG_GRADIENTS = 10_300_000_000
f32, bf16 = jnp.float32, jnp.bfloat16


def swap_cores(block):
    return lax.ppermute(block, "c", [(0, 1), (1, 0)])


def from_xor(block, bits):
    return lax.ppermute(block, "zl", [(i, i ^ bits) for i in range(4)])


def halves(value):
    high = value.astype(bf16)
    return high, (value - high.astype(f32)).astype(bf16)


def call(kernel, name, out_shape, in_specs, out_specs, scratch, cycles):
    return pl.pallas_call(
        kernel,
        out_shape=out_shape,
        in_specs=in_specs,
        out_specs=out_specs,
        scratch_shapes=scratch,
        compiler_params=pltpu.CompilerParams(vmem_limit_bytes=LIMITS.get(name, 8) * 1024 * 1024),
        cost_estimate=pl.CostEstimate(flops=cycles, bytes_accessed=4_000_000, transcendentals=0),
        name=name,
    )


VM, SM, ANY = pl.BlockSpec(memory_space=pltpu.VMEM), pl.BlockSpec(memory_space=pltpu.SMEM), pl.BlockSpec(memory_space=pl.ANY)
CONTRACT = (((1,), (1,)), ((), ()))
BASIS = (16, 4, 16, WIDTH)


def repeat_kernel(block, out):
    for peer in range(16):
        out[peer] = block[...]


def repeat(block):
    shape = jax.ShapeDtypeStruct((16, *block.shape), bf16)
    return call(repeat_kernel, "repeat", shape, [VM], VM, [], SHORT)(block)


def spread_kernel(along_z, out):
    for zl in range(4):
        block = jnp.concatenate([along_z[zh, zl].astype(f32) for zh in range(4)], axis=0).astype(bf16)
        for peer in range(16):
            out[peer, zl] = block


def spread(along_z):
    return call(
        spread_kernel, "spread", jax.ShapeDtypeStruct(BASIS, bf16), [VM], VM, [], LONG
    )(along_z)


def pick_kernel(place, error, act, out, held, sems, done):
    copies, outs = [], []
    for z in range(4):
        start = pl.multiple_of((2 * z + 1 - place[1]) * WIDTH, 128)
        copies.append(pltpu.make_async_copy(error.at[:, pl.ds(start, WIDTH)], held.at[z], sems.at[z]))
    copies.append(pltpu.make_async_copy(act, held.at[4, :, pl.ds(0, TOKENS)], sems.at[4]))
    for copy in copies:
        copy.start()
    held[4, :, TOKENS:] = jnp.zeros((ROWS, WIDTH - TOKENS), bf16)
    for z in range(5):
        copies[z].wait()
        outs.append(pltpu.make_async_copy(held.at[z], out.at[z], done.at[z]))
        outs[z].start()
    for copy in outs:
        copy.wait()


def pick(place, error, act):
    shape = jax.ShapeDtypeStruct((5, ROWS, WIDTH), bf16)
    scratch = [
        pltpu.VMEM((5, ROWS, WIDTH), bf16),
        pltpu.SemaphoreType.DMA((5,)),
        pltpu.SemaphoreType.DMA((5,)),
    ]
    return call(pick_kernel, "pick", shape, [SM, ANY, ANY], ANY, scratch, SHORT)(place, error, act)


def arrived_kernel(first, second, out):
    out[...] = jnp.zeros_like(out)


def arrived(first, second):
    shape = jax.ShapeDtypeStruct((8, 128), f32)
    return call(arrived_kernel, "arrived", shape, [ANY, ANY], VM, [], LONG_GRADIENTS)(first, second)


def start_basis(source, target, sems):
    copies = [pltpu.make_async_copy(source.at[pl.ds(4 * i, 4)], target.at[pl.ds(4 * i, 4)], sems.at[i]) for i in range(4)]
    for copy in copies:
        copy.start()
    return copies


def project_kernel(
    place, act, picked, first, second, third, fourth, error, own, ready, turned, sums, sums_sent, total, total_sent,
    acts, grads, errors, basis, totals, sems, basis_sems, act_sems, done,
):
    zl, core = place[0], place[1]
    heads = [
        pltpu.make_async_copy(act, acts.at[0], act_sems.at[0]),
        pltpu.make_async_copy(picked.at[4, :, pl.ds(0, TOKENS)], acts.at[1], act_sems.at[1]),
    ]
    for copy in heads:
        copy.start()
    copies = []
    for bits, source in enumerate((first, second, third, fourth)):
        z = zl ^ bits
        start = pl.multiple_of((2 * z + core) * WIDTH, 128)
        moved = [
            pltpu.make_async_copy(source, grads.at[bits], sems.at[bits, 0]),
            pltpu.make_async_copy(error.at[:, pl.ds(start, WIDTH)], errors.at[0, bits], sems.at[bits, 1]),
            pltpu.make_async_copy(picked.at[z], errors.at[1, bits], sems.at[bits, 2]),
        ]
        for copy in moved:
            copy.start()
        copies.append(moved)
    halves_of_basis = start_basis(own, basis, basis_sems)
    for copy in heads:
        copy.wait()
    outs = []
    for bits in range(4):
        for copy in copies[bits]:
            copy.wait()
        for side in range(2):
            gradient = jnp.dot(acts[side], grads[bits], preferred_element_type=f32).astype(bf16)
            high, low = halves(gradient.astype(f32) + errors[side, bits].astype(f32))
            totals[bits, side, :ROWS] = high
            totals[bits, side, ROWS:] = low
            target = (total_sent if side else total).at[zl ^ bits]
            outs.append(pltpu.make_async_copy(totals.at[bits, side], target, done.at[bits, side]))
            outs[-1].start()
    for copy in halves_of_basis:
        copy.wait()
    values = [jnp.zeros((2 * ROWS, RANK), f32)] * 2
    for bits in range(4):
        part = basis[:, zl ^ bits].reshape(RANK, WIDTH)
        for side in range(2):
            values[side] += lax.dot_general(totals[bits, side], part, CONTRACT, preferred_element_type=f32)
    for side in range(2):
        projected = values[side][:ROWS] + values[side][ROWS:]
        (sums_sent if side else sums)[...] = projected
        padded = jnp.concatenate([projected, jnp.zeros((RANK - ROWS, RANK), f32)], axis=0)
        turned[1 - core if side else core] = padded.T[:, :ROWS].astype(bf16)
    for copy in outs:
        copy.wait()


def project(place, act, picked, grads, error, own, ready):
    return call(
        project_kernel,
        "project",
        (
            jax.ShapeDtypeStruct((2, RANK, ROWS), bf16),
            jax.ShapeDtypeStruct((ROWS, RANK), f32),
            jax.ShapeDtypeStruct((ROWS, RANK), f32),
            jax.ShapeDtypeStruct((4, 2 * ROWS, WIDTH), bf16),
            jax.ShapeDtypeStruct((4, 2 * ROWS, WIDTH), bf16),
        ),
        [SM] + [ANY] * 8 + [VM],
        (VM, VM, VM, ANY, ANY),
        [
            pltpu.VMEM((2, ROWS, TOKENS), bf16),
            pltpu.VMEM((4, TOKENS, WIDTH), bf16),
            pltpu.VMEM((2, 4, ROWS, WIDTH), bf16),
            pltpu.VMEM(BASIS, bf16),
            pltpu.VMEM((4, 2, 2 * ROWS, WIDTH), bf16),
            pltpu.SemaphoreType.DMA((4, 3)),
            pltpu.SemaphoreType.DMA((4,)),
            pltpu.SemaphoreType.DMA((2,)),
            pltpu.SemaphoreType.DMA((4, 2)),
        ],
        SHORT,
    )(place, act, picked, *grads, error, own, ready)


def feedback_kernel(
    blocks, place, total, total_other, sums, received, own, other, *rest
):
    out, totals, basis, results, sems, basis_sems, done = rest[-7:]
    core = place[1]
    copies, moved = [], []
    for side, source in enumerate((own, other)):
        for i in range(4):
            peers = pl.ds(4 * i, 4)
            half = source.at[peers, pl.ds(blocks[0], 2)]
            copies.append(pltpu.make_async_copy(half, basis.at[side, peers], basis_sems.at[side, i]))
            copies[-1].start()
    for i, z in enumerate(blocks):
        for side, source in enumerate((total, total_other)):
            moved.append(pltpu.make_async_copy(source.at[z], totals.at[i, side], sems.at[i, side]))
            moved[-1].start()
    backs = jnp.concatenate(halves(sums[...] + received[...]), axis=0)
    for copy in copies:
        copy.wait()
    outs = []
    for i, z in enumerate(blocks):
        for side in range(2):
            moved[2 * i + side].wait()
            part = basis[side, :, i].reshape(RANK, WIDTH)
            back = jnp.dot(backs, part, preferred_element_type=f32)
            value = totals[i, side, :ROWS].astype(f32) + totals[i, side, ROWS:].astype(f32)
            results[i, side] = (value - (back[:ROWS] + back[ROWS:])).astype(bf16)
            start = pl.multiple_of((2 * z + (1 - core if side else core)) * WIDTH, 128)
            outs.append(pltpu.make_async_copy(results.at[i, side], out.at[:, pl.ds(start, WIDTH)], done.at[i, side]))
            outs[-1].start()
    for copy in outs:
        copy.wait()


def feedback(blocks, begun, place, total, total_other, sums, received, own, other):
    operands = (place, total, total_other, sums, received, own, other)
    in_specs = [SM, ANY, ANY, VM, VM, ANY, ANY]
    aliases = {}
    if begun is not None:
        operands, in_specs, aliases = (*operands, begun), in_specs + [ANY], {7: 0}
    return pl.pallas_call(
        functools.partial(feedback_kernel, blocks),
        out_shape=jax.ShapeDtypeStruct((ROWS, COLUMNS), bf16),
        in_specs=in_specs,
        out_specs=ANY,
        scratch_shapes=[
            pltpu.VMEM((2, 2, 2 * ROWS, WIDTH), bf16),
            pltpu.VMEM((2, 16, 2, 16, WIDTH), bf16),
            pltpu.VMEM((2, 2, ROWS, WIDTH), bf16),
            pltpu.SemaphoreType.DMA((2, 2)),
            pltpu.SemaphoreType.DMA((2, 4)),
            pltpu.SemaphoreType.DMA((2, 2)),
        ],
        input_output_aliases=aliases,
        compiler_params=pltpu.CompilerParams(vmem_limit_bytes=LIMITS["feedback"] * 1024 * 1024),
        cost_estimate=pl.CostEstimate(flops=LONG_FEEDBACK, bytes_accessed=4_000_000, transcendentals=0),
        name="feedback",
    )(*operands)


def weight_kernel(place, updates, own, other, out, held, mine, theirs, results, head, sems, done):
    first = place[1] == 0
    head_copy = pltpu.make_async_copy(updates, held, head.at[0])
    head_copy.start()
    copies = start_basis(own, mine, sems.at[0]) + start_basis(other, theirs, sems.at[1])
    head_copy.wait()
    value = held[...].reshape(RANK, ROWS).astype(f32)
    padded = jnp.concatenate([value, jnp.zeros((RANK, RANK - ROWS), f32)], axis=1)
    turned = padded.T[:ROWS].astype(bf16)
    for copy in copies:
        copy.wait()
    outs = []
    for z in range(4):
        both = mine[:, z].reshape(RANK, WIDTH), theirs[:, z].reshape(RANK, WIDTH)
        for core in range(2):
            part = jnp.where(first, both[core], both[1 - core])
            start = (2 * z + core) * WIDTH
            step = jnp.dot(turned, part, preferred_element_type=f32)
            results[:, start : start + WIDTH] = step.astype(bf16)
        columns = pl.ds(z * 2 * WIDTH, 2 * WIDTH)
        outs.append(pltpu.make_async_copy(results.at[:, columns], out.at[:, columns], done.at[z]))
        outs[z].start()
    for copy in outs:
        copy.wait()


def weight(place, updates, own, other):
    return call(
        weight_kernel,
        "weight_step",
        jax.ShapeDtypeStruct((ROWS, COLUMNS), bf16),
        [SM, ANY, ANY, ANY],
        ANY,
        [
            pltpu.VMEM((16, 16, ROWS), bf16),
            pltpu.VMEM(BASIS, bf16),
            pltpu.VMEM(BASIS, bf16),
            pltpu.VMEM((ROWS, COLUMNS), bf16),
            pltpu.SemaphoreType.DMA((1,)),
            pltpu.SemaphoreType.DMA((2, 4)),
            pltpu.SemaphoreType.DMA((4,)),
        ],
        SHORT,
    )(place, updates, own, other)


def combine_kernel(part, first, second, out):
    total = jnp.sum(part[...].astype(f32), axis=0)
    for peer in range(4):
        out[peer, :16] = total
        out[peer, 16:20] = first[...]
        out[peer, 20:] = second[...]


def combine(part, first, second):
    shape = jax.ShapeDtypeStruct((4, 24, ROWS), f32)
    return call(combine_kernel, "combine", shape, [VM] * 3, VM, [], LONG_COMBINE)(part, first, second)


def moments(first, second, mean):
    first = BETA_ONE * first + (1.0 - BETA_ONE) * mean
    second = BETA_TWO * second + (1.0 - BETA_TWO) * mean * mean
    return first, second


def update_kernel(place, both, out, first_own, second_own, held):
    mean = (both[0, :16] + both[1, :16] + both[2, :16] + both[3, :16]) / 64
    for peer in range(4):
        held[peer] = mean[4 * peer : 4 * peer + 4]
    first = jnp.concatenate([both[peer, 16:20] for peer in range(4)], axis=0)
    second = jnp.concatenate([both[peer, 20:24] for peer in range(4)], axis=0)
    first, second = moments(first, second, mean)
    first_hat = first / (1.0 - BETA_ONE**STEP)
    second_hat = second / (1.0 - BETA_TWO**STEP)
    update = (first_hat / (jnp.sqrt(second_hat) + EPSILON)).astype(bf16)
    for peer in range(16):
        out[peer] = update
    zh = place[2]
    mine = held[zh]
    first_own[...], second_own[...] = moments(both[zh, 16:20], both[zh, 20:24], mine)


def new_update(place, both):
    shape = jax.ShapeDtypeStruct((4, ROWS), f32)
    return call(
        update_kernel,
        "update",
        (jax.ShapeDtypeStruct((16, 16, ROWS), bf16), shape, shape),
        [SM, VM],
        (VM, VM, VM),
        [pltpu.VMEM((4, 4, ROWS), f32)],
        LONG_UPDATE,
    )(place, both)


def local(hidden_act, out_grad, error_in, subspace, first_moment, second_moment):
    zh = lax.axis_index("zh")
    place = jnp.stack([lax.axis_index("zl"), lax.axis_index("c"), zh]).astype(jnp.int32)
    act = hidden_act.T

    along_z = lax.all_to_all(repeat(subspace.T), ("zh", "zl"), 0, 0)
    spreading = spread(along_z.reshape(4, 4, 4, WIDTH))
    own = lax.all_to_all(spreading, ("x", "y"), 0, 0)
    error = error_in[0]
    error = error_in[0]
    grads = [out_grad] + [from_xor(out_grad, bits) for bits in (1, 2, 3)]
    picked = swap_cores(pick(place, error, act))
    ready = arrived(grads[2], grads[3])
    own, ready, picked, grads[1] = lax.optimization_barrier((own, ready, picked, grads[1]))
    turned, sums, sums_sent, total, total_sent = project(place, act, picked, grads, error, own, ready)

    part = lax.all_to_all(turned.reshape(32, 16, ROWS), ("c", "x", "y"), 0, 0)
    received, total_other, other = swap_cores(sums_sent), swap_cores(total_sent), swap_cores(own)
    both = combine(part, first_moment.T, second_moment.T)
    both = lax.all_to_all(both, "zh", 0, 0)
    needed = place, total, total_other, sums, received, own, other
    begun = feedback((0, 1), None, *needed)
    both, begun = lax.optimization_barrier((both, begun))
    error_out = feedback((2, 3), begun, *needed)
    update, first_own, second_own = new_update(place, both)
    updates = lax.all_to_all(update, ("x", "y"), 0, 0)
    weight_step = weight(place, updates, own, other)
    return (weight_step, error_out[None], first_own.T, second_own.T)


def solution(mesh):
    fine = Mesh(mesh.devices.reshape(SIZES), AXES)
    placed = (
        P(DP, TENSOR),
        P(DP, TENSOR),
        P(DP, TENSOR, None),
        P(TENSOR, DP),
        P(TENSOR, DP),
        P(TENSOR, DP),
    )
    return jax.shard_map(
        local,
        mesh=fine,
        in_specs=placed,
        out_specs=(P(TENSOR, None), P(DP, TENSOR, None), P(TENSOR, DP), P(TENSOR, DP)),
        check_vma=False,
    )
```

```python
import functools

import jax
import jax.numpy as jnp
from jax import lax
from jax.experimental import pallas as pl
from jax.experimental.pallas import tpu as pltpu
from jax.sharding import Mesh, PartitionSpec as P

STEP = 20
BETA_ONE = 0.9
BETA_TWO = 0.999
EPSILON = 1e-08

AXES = ("zh", "x", "y", "zl", "c")
SIZES = (4, 4, 4, 4, 2)
DP = ("zh", "x", "y")
TENSOR = ("zl", "c")
ROWS, WIDTH, RANK, TOKENS = 144, 640, 256, 256
COLUMNS = 8 * WIDTH
LIMITS = {"project": 50, "feedback": 50, "weight_step": 24}
LONG = 60_000_000_000
SHORT = 1_000_000_000
LONG_COMBINE = 17_000_000_000
LONG_UPDATE = 1_000_000_000
LONG_FEEDBACK = 1_000_000_000
LONG_GRADIENTS = 12_000_000_000
f32, bf16 = jnp.float32, jnp.bfloat16


def swap_cores(block):
    return lax.ppermute(block, "c", [(0, 1), (1, 0)])


def from_xor(block, bits):
    return lax.ppermute(block, "zl", [(i, i ^ bits) for i in range(4)])


def halves(value):
    high = value.astype(bf16)
    return high, (value - high.astype(f32)).astype(bf16)


def call(kernel, name, out_shape, in_specs, out_specs, scratch, cycles):
    return pl.pallas_call(
        kernel,
        out_shape=out_shape,
        in_specs=in_specs,
        out_specs=out_specs,
        scratch_shapes=scratch,
        compiler_params=pltpu.CompilerParams(vmem_limit_bytes=LIMITS.get(name, 8) * 1024 * 1024),
        cost_estimate=pl.CostEstimate(flops=cycles, bytes_accessed=4_000_000, transcendentals=0),
        name=name,
    )


VM, SM, ANY = pl.BlockSpec(memory_space=pltpu.VMEM), pl.BlockSpec(memory_space=pltpu.SMEM), pl.BlockSpec(memory_space=pl.ANY)
CONTRACT = (((1,), (1,)), ((), ()))
BASIS = (16, 4, 16, WIDTH)


def repeat_kernel(block, out):
    for peer in range(16):
        out[peer] = block[...]


def repeat(block):
    shape = jax.ShapeDtypeStruct((16, *block.shape), bf16)
    return call(repeat_kernel, "repeat", shape, [VM], VM, [], SHORT)(block)


def spread_kernel(along_z, out):
    for zl in range(4):
        block = jnp.concatenate([along_z[zh, zl].astype(f32) for zh in range(4)], axis=0).astype(bf16)
        for peer in range(16):
            out[peer, zl] = block


def spread(along_z):
    return call(
        spread_kernel, "spread", jax.ShapeDtypeStruct(BASIS, bf16), [VM], VM, [], LONG
    )(along_z)


def pick_kernel(place, error, act, out, held, sems, done):
    copies, outs = [], []
    for z in range(4):
        start = pl.multiple_of((2 * z + 1 - place[1]) * WIDTH, 128)
        copies.append(pltpu.make_async_copy(error.at[:, pl.ds(start, WIDTH)], held.at[z], sems.at[z]))
    copies.append(pltpu.make_async_copy(act, held.at[4, :, pl.ds(0, TOKENS)], sems.at[4]))
    for copy in copies:
        copy.start()
    held[4, :, TOKENS:] = jnp.zeros((ROWS, WIDTH - TOKENS), bf16)
    for z in range(5):
        copies[z].wait()
        outs.append(pltpu.make_async_copy(held.at[z], out.at[z], done.at[z]))
        outs[z].start()
    for copy in outs:
        copy.wait()


def pick(place, error, act):
    shape = jax.ShapeDtypeStruct((5, ROWS, WIDTH), bf16)
    scratch = [
        pltpu.VMEM((5, ROWS, WIDTH), bf16),
        pltpu.SemaphoreType.DMA((5,)),
        pltpu.SemaphoreType.DMA((5,)),
    ]
    return call(pick_kernel, "pick", shape, [SM, ANY, ANY], ANY, scratch, SHORT)(place, error, act)


def arrived_kernel(first, second, out):
    out[...] = jnp.zeros_like(out)


def arrived(first, second):
    shape = jax.ShapeDtypeStruct((8, 128), f32)
    return call(arrived_kernel, "arrived", shape, [ANY, ANY], VM, [], LONG_GRADIENTS)(first, second)


def start_basis(source, target, sems):
    copies = [pltpu.make_async_copy(source.at[pl.ds(4 * i, 4)], target.at[pl.ds(4 * i, 4)], sems.at[i]) for i in range(4)]
    for copy in copies:
        copy.start()
    return copies


def project_kernel(
    place, act, picked, first, second, third, fourth, error, own, ready, turned, sums, sums_sent, total, total_sent,
    acts, grads, errors, basis, totals, sems, basis_sems, act_sems, done,
):
    zl, core = place[0], place[1]
    heads = [
        pltpu.make_async_copy(act, acts.at[0], act_sems.at[0]),
        pltpu.make_async_copy(picked.at[4, :, pl.ds(0, TOKENS)], acts.at[1], act_sems.at[1]),
    ]
    for copy in heads:
        copy.start()
    copies = []
    for bits, source in enumerate((first, second, third, fourth)):
        z = zl ^ bits
        start = pl.multiple_of((2 * z + core) * WIDTH, 128)
        moved = [
            pltpu.make_async_copy(source, grads.at[bits], sems.at[bits, 0]),
            pltpu.make_async_copy(error.at[:, pl.ds(start, WIDTH)], errors.at[0, bits], sems.at[bits, 1]),
            pltpu.make_async_copy(picked.at[z], errors.at[1, bits], sems.at[bits, 2]),
        ]
        for copy in moved:
            copy.start()
        copies.append(moved)
    halves_of_basis = start_basis(own, basis, basis_sems)
    for copy in heads:
        copy.wait()
    outs = []
    for bits in range(4):
        for copy in copies[bits]:
            copy.wait()
        for side in range(2):
            gradient = jnp.dot(acts[side], grads[bits], preferred_element_type=f32).astype(bf16)
            high, low = halves(gradient.astype(f32) + errors[side, bits].astype(f32))
            totals[bits, side, :ROWS] = high
            totals[bits, side, ROWS:] = low
            target = (total_sent if side else total).at[zl ^ bits]
            outs.append(pltpu.make_async_copy(totals.at[bits, side], target, done.at[bits, side]))
            outs[-1].start()
    for copy in halves_of_basis:
        copy.wait()
    values = [jnp.zeros((2 * ROWS, RANK), f32)] * 2
    for bits in range(4):
        part = basis[:, zl ^ bits].reshape(RANK, WIDTH)
        for side in range(2):
            values[side] += lax.dot_general(totals[bits, side], part, CONTRACT, preferred_element_type=f32)
    for side in range(2):
        projected = values[side][:ROWS] + values[side][ROWS:]
        (sums_sent if side else sums)[...] = projected
        padded = jnp.concatenate([projected, jnp.zeros((RANK - ROWS, RANK), f32)], axis=0)
        turned[1 - core if side else core] = padded.T[:, :ROWS].astype(bf16)
    for copy in outs:
        copy.wait()


def project(place, act, picked, grads, error, own, ready):
    return call(
        project_kernel,
        "project",
        (
            jax.ShapeDtypeStruct((2, RANK, ROWS), bf16),
            jax.ShapeDtypeStruct((ROWS, RANK), f32),
            jax.ShapeDtypeStruct((ROWS, RANK), f32),
            jax.ShapeDtypeStruct((4, 2 * ROWS, WIDTH), bf16),
            jax.ShapeDtypeStruct((4, 2 * ROWS, WIDTH), bf16),
        ),
        [SM] + [ANY] * 8 + [VM],
        (VM, VM, VM, ANY, ANY),
        [
            pltpu.VMEM((2, ROWS, TOKENS), bf16),
            pltpu.VMEM((4, TOKENS, WIDTH), bf16),
            pltpu.VMEM((2, 4, ROWS, WIDTH), bf16),
            pltpu.VMEM(BASIS, bf16),
            pltpu.VMEM((4, 2, 2 * ROWS, WIDTH), bf16),
            pltpu.SemaphoreType.DMA((4, 3)),
            pltpu.SemaphoreType.DMA((4,)),
            pltpu.SemaphoreType.DMA((2,)),
            pltpu.SemaphoreType.DMA((4, 2)),
        ],
        SHORT,
    )(place, act, picked, *grads, error, own, ready)


def feedback_kernel(
    blocks, place, total, total_other, sums, received, own, other, *rest
):
    out, totals, basis, results, sems, basis_sems, done = rest[-7:]
    core = place[1]
    copies, moved = [], []
    for side, source in enumerate((own, other)):
        for i in range(4):
            peers = pl.ds(4 * i, 4)
            half = source.at[peers, pl.ds(blocks[0], 2)]
            copies.append(pltpu.make_async_copy(half, basis.at[side, peers], basis_sems.at[side, i]))
            copies[-1].start()
    for i, z in enumerate(blocks):
        for side, source in enumerate((total, total_other)):
            moved.append(pltpu.make_async_copy(source.at[z], totals.at[i, side], sems.at[i, side]))
            moved[-1].start()
    backs = jnp.concatenate(halves(sums[...] + received[...]), axis=0)
    for copy in copies:
        copy.wait()
    outs = []
    for i, z in enumerate(blocks):
        for side in range(2):
            moved[2 * i + side].wait()
            part = basis[side, :, i].reshape(RANK, WIDTH)
            back = jnp.dot(backs, part, preferred_element_type=f32)
            value = totals[i, side, :ROWS].astype(f32) + totals[i, side, ROWS:].astype(f32)
            results[i, side] = (value - (back[:ROWS] + back[ROWS:])).astype(bf16)
            start = pl.multiple_of((2 * z + (1 - core if side else core)) * WIDTH, 128)
            outs.append(pltpu.make_async_copy(results.at[i, side], out.at[:, pl.ds(start, WIDTH)], done.at[i, side]))
            outs[-1].start()
    for copy in outs:
        copy.wait()


def feedback(blocks, begun, place, total, total_other, sums, received, own, other):
    operands = (place, total, total_other, sums, received, own, other)
    in_specs = [SM, ANY, ANY, VM, VM, ANY, ANY]
    aliases = {}
    if begun is not None:
        operands, in_specs, aliases = (*operands, begun), in_specs + [ANY], {7: 0}
    return pl.pallas_call(
        functools.partial(feedback_kernel, blocks),
        out_shape=jax.ShapeDtypeStruct((ROWS, COLUMNS), bf16),
        in_specs=in_specs,
        out_specs=ANY,
        scratch_shapes=[
            pltpu.VMEM((2, 2, 2 * ROWS, WIDTH), bf16),
            pltpu.VMEM((2, 16, 2, 16, WIDTH), bf16),
            pltpu.VMEM((2, 2, ROWS, WIDTH), bf16),
            pltpu.SemaphoreType.DMA((2, 2)),
            pltpu.SemaphoreType.DMA((2, 4)),
            pltpu.SemaphoreType.DMA((2, 2)),
        ],
        input_output_aliases=aliases,
        compiler_params=pltpu.CompilerParams(vmem_limit_bytes=LIMITS["feedback"] * 1024 * 1024),
        cost_estimate=pl.CostEstimate(flops=LONG_FEEDBACK, bytes_accessed=4_000_000, transcendentals=0),
        name="feedback",
    )(*operands)


def weight_kernel(place, updates, own, other, out, held, mine, theirs, results, head, sems, done):
    first = place[1] == 0
    head_copy = pltpu.make_async_copy(updates, held, head.at[0])
    head_copy.start()
    copies = start_basis(own, mine, sems.at[0]) + start_basis(other, theirs, sems.at[1])
    head_copy.wait()
    value = held[...].reshape(RANK, ROWS).astype(f32)
    padded = jnp.concatenate([value, jnp.zeros((RANK, RANK - ROWS), f32)], axis=1)
    turned = padded.T[:ROWS].astype(bf16)
    for copy in copies:
        copy.wait()
    outs = []
    for z in range(4):
        both = mine[:, z].reshape(RANK, WIDTH), theirs[:, z].reshape(RANK, WIDTH)
        for core in range(2):
            part = jnp.where(first, both[core], both[1 - core])
            start = (2 * z + core) * WIDTH
            step = jnp.dot(turned, part, preferred_element_type=f32)
            results[:, start : start + WIDTH] = step.astype(bf16)
        columns = pl.ds(z * 2 * WIDTH, 2 * WIDTH)
        outs.append(pltpu.make_async_copy(results.at[:, columns], out.at[:, columns], done.at[z]))
        outs[z].start()
    for copy in outs:
        copy.wait()


def weight(place, updates, own, other):
    return call(
        weight_kernel,
        "weight_step",
        jax.ShapeDtypeStruct((ROWS, COLUMNS), bf16),
        [SM, ANY, ANY, ANY],
        ANY,
        [
            pltpu.VMEM((16, 16, ROWS), bf16),
            pltpu.VMEM(BASIS, bf16),
            pltpu.VMEM(BASIS, bf16),
            pltpu.VMEM((ROWS, COLUMNS), bf16),
            pltpu.SemaphoreType.DMA((1,)),
            pltpu.SemaphoreType.DMA((2, 4)),
            pltpu.SemaphoreType.DMA((4,)),
        ],
        SHORT,
    )(place, updates, own, other)


def combine_kernel(part, first, second, out):
    total = jnp.sum(part[...].astype(f32), axis=0)
    for peer in range(4):
        out[peer, :16] = total
        out[peer, 16:20] = first[...]
        out[peer, 20:] = second[...]


def combine(part, first, second):
    shape = jax.ShapeDtypeStruct((4, 24, ROWS), f32)
    return call(combine_kernel, "combine", shape, [VM] * 3, VM, [], LONG_COMBINE)(part, first, second)


def moments(first, second, mean):
    first = BETA_ONE * first + (1.0 - BETA_ONE) * mean
    second = BETA_TWO * second + (1.0 - BETA_TWO) * mean * mean
    return first, second


def update_kernel(place, both, out, first_own, second_own, held):
    mean = (both[0, :16] + both[1, :16] + both[2, :16] + both[3, :16]) / 64
    for peer in range(4):
        held[peer] = mean[4 * peer : 4 * peer + 4]
    first = jnp.concatenate([both[peer, 16:20] for peer in range(4)], axis=0)
    second = jnp.concatenate([both[peer, 20:24] for peer in range(4)], axis=0)
    first, second = moments(first, second, mean)
    first_hat = first / (1.0 - BETA_ONE**STEP)
    second_hat = second / (1.0 - BETA_TWO**STEP)
    update = (first_hat / (jnp.sqrt(second_hat) + EPSILON)).astype(bf16)
    for peer in range(16):
        out[peer] = update
    zh = place[2]
    mine = held[zh]
    first_own[...], second_own[...] = moments(both[zh, 16:20], both[zh, 20:24], mine)


def new_update(place, both):
    shape = jax.ShapeDtypeStruct((4, ROWS), f32)
    return call(
        update_kernel,
        "update",
        (jax.ShapeDtypeStruct((16, 16, ROWS), bf16), shape, shape),
        [SM, VM],
        (VM, VM, VM),
        [pltpu.VMEM((4, 4, ROWS), f32)],
        LONG_UPDATE,
    )(place, both)


def local(hidden_act, out_grad, error_in, subspace, first_moment, second_moment):
    zh = lax.axis_index("zh")
    place = jnp.stack([lax.axis_index("zl"), lax.axis_index("c"), zh]).astype(jnp.int32)
    act = hidden_act.T

    along_z = lax.all_to_all(repeat(subspace.T), ("zh", "zl"), 0, 0)
    spreading = spread(along_z.reshape(4, 4, 4, WIDTH))
    own = lax.all_to_all(spreading, ("x", "y"), 0, 0)
    error = error_in[0]
    error = error_in[0]
    grads = [out_grad] + [from_xor(out_grad, bits) for bits in (1, 2, 3)]
    picked = swap_cores(pick(place, error, act))
    ready = arrived(grads[2], grads[3])
    own, ready, picked, grads[1] = lax.optimization_barrier((own, ready, picked, grads[1]))
    turned, sums, sums_sent, total, total_sent = project(place, act, picked, grads, error, own, ready)

    part = lax.all_to_all(turned.reshape(32, 16, ROWS), ("c", "x", "y"), 0, 0)
    received, total_other, other = swap_cores(sums_sent), swap_cores(total_sent), swap_cores(own)
    both = combine(part, first_moment.T, second_moment.T)
    both = lax.all_to_all(both, "zh", 0, 0)
    needed = place, total, total_other, sums, received, own, other
    begun = feedback((0, 1), None, *needed)
    both, begun = lax.optimization_barrier((both, begun))
    error_out = feedback((2, 3), begun, *needed)
    update, first_own, second_own = new_update(place, both)
    updates = lax.all_to_all(update, ("x", "y"), 0, 0)
    weight_step = weight(place, updates, own, other)
    return (weight_step, error_out[None], first_own.T, second_own.T)


def solution(mesh):
    fine = Mesh(mesh.devices.reshape(SIZES), AXES)
    placed = (
        P(DP, TENSOR),
        P(DP, TENSOR),
        P(DP, TENSOR, None),
        P(TENSOR, DP),
        P(TENSOR, DP),
        P(TENSOR, DP),
    )
    return jax.shard_map(
        local,
        mesh=fine,
        in_specs=placed,
        out_specs=(P(TENSOR, None), P(DP, TENSOR, None), P(TENSOR, DP), P(TENSOR, DP)),
        check_vma=False,
    )
```
